1024 devices in a mesh: row: 16 (over z_hi, y), col: 64 (over z_lo, x, core).
Axes of the slice: x: 4, y: 4, z: 32 (z_hi: 4, z_lo: 8; z = z_hi * 8 + z_lo), core: 2. Of those that a mesh axis runs over, the one named last changes fastest.
Arguments:
- a_blocks: float32 [1024, 128, 128], P(('row', 'col')), may hold values from -0.5 to 0.5
- a_cols: int32 [1024], P(('row', 'col')), may hold values from 0 to 31, as said below
- b_blocks: float32 [32, 64, 128, 128], P('row', 'col'), may hold values from -6 to 6
- b_rows: int32 [32, 64], P('row', 'col'), may hold values from 0 to 31, as said below
- c_rows: int32 [12288], P(('row', 'col')), may hold values from 0 to 127, as said below
- c_cols: int32 [12288], P(('row', 'col')), may hold values from 0 to 255, as said below
Outputs:
- c_blocks: float32 [12288, 128, 128], P(('row', 'col'))
The draws below stay inside these ranges and needn't reach their ends.
Inputs may be any that keep to these rules, and one draw needn't show every extreme that they name: `a_cols`: the 8 indices of one block row of A are distinct and form a run of consecutive indices modulo 32. `b_rows`: the 8 indices of one block column of B are distinct and form a run of consecutive indices modulo 32. The shard on the device with row index r holds block rows r * 8 to (r + 1) * 8 - 1; no pair (c_rows[t], c_cols[t]) repeats; every retained pair has at least one contracted index in common between its row of A and its column of B. `c_cols`: the shard on the device with col index c holds block columns c * 4 to (c + 1) * 4 - 1.
All inputs are finite; a program needn't handle non-finite values.
Results may differ from the reference program's by a relative error of at most 0.0003.
Values sent between devices are 32-bit elements; how exact they have to be, the bound alone decides.
A program may use at most 64 MiB of HBM per device.

```python
import jax
import jax.numpy as jnp
from jax import lax

BS = 128
KA = 8
KB = 8
KSPAN = 32
RG = 8
CW = 4
TC = 12
MR = 128
NBC = 256
N_ROW = 16
N_COL = 64


def a_pattern(key):
    key = jax.random.fold_in(key, 11)
    first, second = jax.random.split(key)
    index = jnp.arange(MR, dtype=jnp.int32)
    anchor = index % RG * N_ROW + index // RG
    jitter = jax.random.randint(first, (MR,), 0, 2).astype(jnp.int32)
    centre = anchor * KSPAN // MR + jitter
    orders = jax.vmap(lambda single: jax.random.permutation(single, KA))(jax.random.split(second, MR)).astype(jnp.int32)
    return (centre[:, None] - KA // 2 + orders) % KSPAN


def b_pattern(key):
    key = jax.random.fold_in(key, 23)
    first, second = jax.random.split(key)
    index = jnp.arange(NBC, dtype=jnp.int32)
    anchor = index % CW * N_COL + index // CW
    jitter = jax.random.randint(first, (NBC,), 0, 2).astype(jnp.int32)
    centre = anchor * KSPAN // NBC + jitter
    orders = jax.vmap(lambda single: jax.random.permutation(single, KB))(jax.random.split(second, NBC)).astype(jnp.int32)
    return (centre[:, None] - KB // 2 + orders) % KSPAN


def target_pairs(key):
    a_keys = a_pattern(key).reshape(N_ROW, 1, RG, 1, KA, 1)
    b_keys = b_pattern(key).reshape(1, N_COL, 1, CW, 1, KB)
    counts = jnp.sum((a_keys == b_keys).astype(jnp.int32), axis=(4, 5)).reshape(N_ROW * N_COL, RG * CW)
    tiekey = jax.random.fold_in(key, 37)
    ties = jax.vmap(lambda single: jax.random.permutation(single, RG * CW))(jax.random.split(tiekey, N_ROW * N_COL)).astype(jnp.int32)
    scores = (counts > 0).astype(jnp.int32) * (RG * CW) + ties
    picks = jax.lax.top_k(scores, TC)[1].astype(jnp.int32)
    device = jnp.arange(N_ROW * N_COL, dtype=jnp.int32)[:, None]
    target_rows = device // N_COL * RG + picks // CW
    target_cols = device % N_COL * CW + picks % CW
    return (target_rows.reshape(-1), target_cols.reshape(-1))


def draw_c_rows(key, part):
    return target_pairs(key)[0]


def draw_c_cols(key, part):
    return target_pairs(key)[1]


def draw_a_cols(key, part):
    return a_pattern(key).reshape(-1)


def draw_b_rows(key, part):
    pattern = b_pattern(key).reshape(NBC // CW, CW, KB)
    return jnp.transpose(pattern, (1, 2, 0)).reshape(CW * KB, NBC // CW)


def shard_levels(own_key, dims, shards, low, high):
    factor_of, own = 1.0, jax.random.fold_in(own_key, 6)
    for position, shards_of in shards:
        heights = jnp.exp(jax.random.uniform(jax.random.fold_in(own, position), (shards_of,), jnp.float32, low / len(shards), high / len(shards)))
        factor_of = factor_of * jnp.repeat(heights, dims[position] // shards_of).reshape([-1 if axis == position else 1 for axis in range(len(dims))])
    return factor_of


def centred(rng, dims, scale, limit, cuts=(), held_as=jnp.bfloat16):
    values = jax.random.normal(rng, dims, jnp.float32) * scale
    if len(cuts) > 0:
        values = shard_levels(rng, dims, cuts, -0.22, 0.18) * values
    return jnp.clip(values, min=-limit, max=limit).astype(held_as)


def setup_inputs(seed: int = 0) -> dict:
    key_list = jax.random.split(jax.random.key(seed), 7)
    a_blocks = centred(key_list[0], (MR * KA, BS, BS), BS ** -0.5, 0.5, ((0, 1024),), jnp.float32)
    a_cols = draw_a_cols(jax.random.fold_in(key_list[6], 71), 0)
    b_blocks = centred(key_list[2], (CW * KB, NBC // CW, BS, BS), 1.0, 6.0, ((0, 16), (1, 64)), jnp.float32)
    b_rows = draw_b_rows(jax.random.fold_in(key_list[6], 71), 0)
    c_rows = draw_c_rows(jax.random.fold_in(key_list[6], 71), 0)
    c_cols = draw_c_cols(jax.random.fold_in(key_list[6], 71), 0)
    return {"a_blocks": a_blocks, "a_cols": a_cols, "b_blocks": b_blocks, "b_rows": b_rows, "c_rows": c_rows, "c_cols": c_cols}


def reference(a_blocks, a_cols, b_blocks, b_rows, c_rows, c_cols):
    a_rowwise = a_blocks.reshape(MR, KA, BS, BS)
    a_index = a_cols.reshape(MR, KA)
    groups = NBC // CW
    b_colwise = jnp.transpose(b_blocks.reshape(CW, KB, groups, BS, BS), (2, 0, 1, 3, 4)).reshape(NBC, KB, BS, BS)
    b_index = jnp.transpose(b_rows.reshape(CW, KB, groups), (2, 0, 1)).reshape(NBC, KB)

    def single_target(pair):
        target_row = pair[0]
        target_col = pair[1]
        a_stack = a_rowwise[target_row]
        a_keys = a_index[target_row]
        column = b_colwise[target_col]
        column_keys = b_index[target_col]
        matched = (a_keys[:, None] == column_keys[None, :]).astype(jnp.float32)
        chosen = jnp.einsum('sq,qxy->sxy', matched, column, precision=lax.Precision.HIGHEST)
        return jnp.einsum('sxy,syz->xz', a_stack, chosen, precision=lax.Precision.HIGHEST)

    return lax.map(single_target, jnp.stack([c_rows, c_cols], axis=1))
```

```python
import functools

import jax
import jax.numpy as jnp
from jax import lax
from jax.experimental import pallas as pl
from jax.experimental.pallas import tpu as pltpu
from jax.sharding import PartitionSpec as P

MESH = pl.DeviceIdType.MESH
BS = 128
KSPAN = 32
SLOTS = 8
NZH, NY, NZL, NX = 4, 4, 8, 4
CUTS = 2
ORDER = (
    "a0", "b0", "y", "k1", "a1", "b1", "k2", "a2", "b2", "x0", "k3", "a3",
    "b3", "x1", "k4", "c1", "a4", "b4", "c2", "x2", "s0", "a5", "b5", "c3",
    "x3", "s1", "a6", "c4", "x4", "s2", "p0", "n0.0.2", "a7", "c5", "x5", "s3",
    "x6", "s4", "c6", "p1", "p3", "n1.0.4", "n3.0.4", "n0.3.4", "x7", "s5", "s6", "s7",
    "n0.5.7", "n1.5.7", "n3.5.7", "t2", "p2", "w2",
)


def kernel(
    a_cols,
    b_rows,
    c_rows,
    c_cols,
    a_ref,
    b_ref,
    out_ref,
    abuf,
    bbuf,
    ah,
    al,
    lhs_h,
    lhs_l,
    rhs,
    cd,
    akv,
    bkv,
    aks,
    bks,
    first,
    where_is,
    a_recv,
    b_recv,
    az_send,
    ax_send,
    ac_send,
    bz_send,
    by_send,
    k_send,
    k_recv,
    loc,
):
    row, col = lax.axis_index("row"), lax.axis_index("col")
    zh, y = row // NY, row % NY
    zl, x, core = col // (2 * NX), (col // 2) % NX, col % 2

    def at_z(d):
        return (row, ((zl + d) % NZL) * 8 + x * 2 + core)

    def at_x(d):
        return (row, zl * 8 + ((x + d) % NX) * 2 + core)

    def at_core():
        return (row, zl * 8 + x * 2 + 1 - core)

    def at_zh(d):
        return (((zh + d) % NZH) * NY + y, col)

    def at_y(d):
        return (zh * NY + (y + d) % NY, col)

    barrier = pltpu.get_barrier_semaphore()
    partners = [at_z(d) for d in range(1, NZL)] + [at_x(d) for d in range(1, NX)]
    partners += [at_core()] + [at_zh(d) for d in range(1, NZH)] + [at_y(d) for d in range(1, NY)]
    for device in partners:
        pl.semaphore_signal(barrier, inc=1, device_id=device, device_id_type=MESH)
    own = [
        pltpu.make_async_copy(a_ref.at[0], abuf.at[col], loc.at[0]),
        pltpu.make_async_copy(b_ref.at[0, 0], bbuf.at[2 * row], loc.at[1]),
        pltpu.make_async_copy(b_ref.at[1, 0], bbuf.at[2 * row + 1], loc.at[2]),
    ]
    for c in own:
        c.start()
    akv[core * 32 + x * 8 + zl] = jnp.full((1, BS), a_cols[0], jnp.int32)
    lane = lax.broadcasted_iota(jnp.int32, (1, BS), 1)
    bkv[y * 4 + zh] = jnp.where(lane == 0, b_rows[0, 0], b_rows[1, 0])
    ah[64] = jnp.zeros((BS, BS), jnp.bfloat16)
    al[64] = jnp.zeros((BS, BS), jnp.bfloat16)
    with jax.named_scope("entry"):
        for c in own:
            c.wait()
        pl.semaphore_wait(barrier, len(partners))

    ends = []

    def copy(ref, send, recv, device):
        return pltpu.make_async_remote_copy(
            src_ref=ref, dst_ref=ref, send_sem=send, recv_sem=recv, device_id=device, device_id_type=MESH
        )

    def when(cond, f):
        if cond is None:
            f()
        else:
            pl.when(cond)(f)

    def go(make, cond=None):
        when(cond, lambda: make().start())
        ends.append(lambda: when(cond, lambda: make().wait_send()))

    def landed(ref, sem):
        pltpu.make_async_copy(ref, ref, sem).wait()

    def a_landed(slot):
        landed(abuf.at[slot], a_recv.at[slot])

    def a_z(slot, j, d, cond):
        go(lambda: copy(abuf.at[slot], az_send.at[j], a_recv.at[slot], at_z(d)), cond)

    def a_x(slot, j, cond):
        for n, d in enumerate((1, 3, 2)):
            go(lambda n=n, d=d: copy(abuf.at[slot], ax_send.at[3 * j + n], a_recv.at[slot], at_x(d)), cond)

    def a_core(slot, j, cond):
        go(lambda: copy(abuf.at[slot], ac_send.at[j], a_recv.at[slot], at_core()), cond)

    def line(k, sign):
        z = zl + sign * k
        return jnp.clip(z, 0, NZL - 1), (None if k == 0 else (z >= 0) & (z < NZL))

    def sides(k):
        return (0,) if k == 0 else (-1, 1)

    def number(k, sign):
        return 0 if k == 0 else 2 * k - 1 + (sign > 0)

    def a_line(k):
        for sign in sides(k):
            z, valid = line(k, sign)
            slot = z * 8 + x * 2 + core
            if k > 0:
                when(valid, lambda: a_landed(slot))
            more_right = (zl < NZL - 1) if valid is None else valid & (zl < NZL - 1)
            more_left = (zl > 0) if valid is None else valid & (zl > 0)
            if sign <= 0 and k < NZL - 1:
                a_z(slot, k, 1, more_right)
            if sign >= 0 and k < NZL - 1:
                a_z(slot, 8 + k, -1, more_left)
        for sign in sides(k):
            z, valid = line(k, sign)
            slot = z * 8 + x * 2 + core
            a_x(slot, number(k, sign), valid)
            a_core(slot, number(k, sign), valid)

    def a_from_x(k):
        for sign in sides(k):
            z, valid = line(k, sign)
            for n, d in enumerate((3, 1, 2)):
                slot = z * 8 + ((x + d) % NX) * 2 + core
                when(valid, lambda: a_landed(slot))
                a_core(slot, 16 + 3 * number(k, sign) + n, valid)

    def a_split(k):
        for sign in sides(k):
            z, valid = line(k, sign)

            def whole():
                for n in range(NX):
                    a_landed(z * 8 + n * 2 + 1 - core)

                def one(s, carry):
                    v = abuf[z * 8 + s]
                    hi = v.astype(jnp.bfloat16)
                    ah[z * 8 + s] = hi
                    al[z * 8 + s] = (v - hi.astype(jnp.float32)).astype(jnp.bfloat16)
                    return carry

                lax.fori_loop(0, SLOTS, one, 0)

            when(valid, whole)

    part = BS // CUTS

    def b_piece(q, i, h):
        return bbuf.at[2 * (((zh + q) % NZH) * NY + y) + i, pl.ds(h * part, part)]

    def b_sem(q, i, h):
        return b_recv.at[2 * (((zh + q) % NZH) * NY + y) + i, h]

    def b_z(q, i, h, d, j):
        return lambda: copy(b_piece(q, i, h), bz_send.at[j], b_sem(q, i, h), at_zh(d))

    state = {"come": 0, "y": 0}

    def b_y(q, i, h):
        for d in (1, 3, 2):
            j = state["y"]
            go(lambda j=j, d=d: copy(b_piece(q, i, h), by_send.at[j], b_sem(q, i, h), at_y(d)))
            state["y"] += 1

    to_right = [(0, i, h) for i in (0, 1) for h in range(CUTS)] + [(-1, 0, h) for h in range(CUTS)]
    to_left = [(0, i, h) for i in (1, 0) for h in range(CUTS)] + [(1, 1, h) for h in range(CUTS)]
    from_left = [(-1, i, h) for i in (0, 1) for h in range(CUTS)] + [(2, 0, h) for h in range(CUTS)]
    from_right = [(1, i, h) for i in (1, 0) for h in range(CUTS)] + [(2, 1, h) for h in range(CUTS)]

    def b_come(count):
        while state["come"] < count:
            for p in (from_left[state["come"]], from_right[state["come"]]):
                landed(b_piece(*p), b_sem(*p))
                b_y(*p)
            state["come"] += 1

    def b_send(k):
        go(b_z(*to_right[k], 1, 2 * k))
        go(b_z(*to_left[k], 3, 2 * k + 1))

    def b_own_y():
        for i in (0, 1):
            for h in range(CUTS):
                b_y(0, i, h)

    sems = {"n": 0}

    def key_go(ref, back, device):
        j = sems["n"]
        sems["n"] += 1
        go(lambda: copy(ref, k_send.at[j], k_recv.at[j], device))
        return lambda: landed(back, k_recv.at[j])

    def keys_1():
        out = []
        for d in range(1, NZL):
            base = core * 32 + x * 8
            out.append(key_go(akv.at[base + zl], akv.at[base + (zl - d) % NZL], at_z(d)))
        for d in range(1, NZH):
            out.append(key_go(bkv.at[y * 4 + zh], bkv.at[y * 4 + (zh - d) % NZH], at_zh(d)))
        return out

    def keys_2():
        out = []
        for d in range(1, NX):
            base = core * 32
            out.append(key_go(akv.at[pl.ds(base + x * 8, 8)], akv.at[pl.ds(base + ((x - d) % NX) * 8, 8)], at_x(d)))
        for d in range(1, NY):
            out.append(key_go(bkv.at[pl.ds(y * 4, 4)], bkv.at[pl.ds(((y - d) % NY) * 4, 4)], at_y(d)))
        return out

    def keys_3():
        return [key_go(akv.at[pl.ds(core * 32, 32)], akv.at[pl.ds((1 - core) * 32, 32)], at_core())]

    def keys_read():
        c0 = pltpu.make_async_copy(akv, aks, loc.at[3])
        c1 = pltpu.make_async_copy(bkv, bks, loc.at[4])
        c0.start()
        c1.start()
        c0.wait()
        c1.wait()

        def one(i, carry):
            keys = [aks[(s % 2) * 32 + (s // 2) * 8 + i, 0, 0] for s in range(SLOTS)]
            past = [lax.rem(k - keys[0] + KSPAN + KSPAN // 2, KSPAN) for k in keys]
            low = functools.reduce(jnp.minimum, past)
            first[i] = lax.rem(keys[0] + low + KSPAN - KSPAN // 2, KSPAN)
            for p in range(SLOTS):
                slot = sum(jnp.where(past[s] - low == p, s, 0) for s in range(SLOTS))
                where_is[i * 9 + p] = i * SLOTS + jnp.minimum(slot, SLOTS - 1)
            where_is[i * 9 + SLOTS] = 64
            return carry

        lax.fori_loop(0, 8, one, 0)

    def column_split(q):
        j = (zh + q) % NZH
        with jax.named_scope(f"column_wait{q}"):
            for d in range(1, NY):
                for i in (0, 1):
                    for h in range(CUTS):
                        slot = 2 * (j * NY + (y + d) % NY) + i
                        landed(bbuf.at[slot, pl.ds(h * part, part)], b_recv.at[slot, h])

        def one(s, carry):
            v = bbuf[j * SLOTS + s]
            hi = v.astype(jnp.bfloat16)
            rows = pl.ds(pl.multiple_of(s * BS, BS), BS)
            rhs[q, rows, :BS] = hi
            rhs[q, rows, BS:] = (v - hi.astype(jnp.float32)).astype(jnp.bfloat16)
            return carry

        lax.fori_loop(0, SLOTS, one, 0)

    def strip(q, i):
        j = (zh + q) % NZH
        rows = pl.ds(pl.multiple_of(i * BS, BS), BS)
        for s in range(SLOTS):
            key = bks[(s // 2) * 4 + j, 0, s % 2]
            at = where_is[i * 9 + jnp.minimum(lax.rem(key - first[i] + KSPAN, KSPAN), SLOTS)]
            lhs_h[rows, s * BS : (s + 1) * BS] = ah[at]
            lhs_l[rows, s * BS : (s + 1) * BS] = al[at]

    def multiply(q, i, count):
        j = (zh + q) % NZH
        rows = pl.ds(pl.multiple_of(i * BS, BS), count * BS)
        wide = jnp.dot(lhs_h[rows, :], rhs[q], preferred_element_type=jnp.float32)
        low = jnp.dot(lhs_l[rows, :], rhs[q, :, :BS], preferred_element_type=jnp.float32)
        total = wide[:, :BS] + wide[:, BS:] + low
        for n in range(count):
            cd[j * 8 + i + n] = total[n * BS : (n + 1) * BS]

    def strips(q):
        def one(i, carry):
            strip(q, i)
            return carry

        with jax.named_scope(f"strips{q}"):
            lax.fori_loop(0, 8, one, 0)

    def whole(q):
        def one(m, carry):
            multiply(q, 2 * m, 2)
            return carry

        with jax.named_scope(f"multiply{q}"):
            lax.fori_loop(0, 4, one, 0)

    def near(q, low, high):
        def one(i, carry):
            away = jnp.abs(i - zl)

            @pl.when((away >= low) & (away <= high))
            def _():
                strip(q, i)
                multiply(q, i, 1)

            return carry

        lax.fori_loop(0, 8, one, 0)

    steps = {
        "a": a_line,
        "x": a_from_x,
        "s": a_split,
        "b": b_send,
        "c": b_come,
        "y": b_own_y,
        "p": column_split,
        "n": near,
        "t": strips,
        "w": whole,
    }
    keys = []
    for step in ORDER:
        if step[0] == "k":
            for f in keys:
                f()
            keys = {"1": keys_1, "2": keys_2, "3": keys_3, "4": keys_read}[step[1]]() or []
        else:
            steps[step[0]](*[int(v) for v in step[1:].split(".") if v])

    def result(t, carry):
        out_ref[t] = cd[lax.rem(c_cols[t], 4) * 8 + lax.rem(c_rows[t], 8)]
        return carry

    with jax.named_scope("result"):
        lax.fori_loop(0, out_ref.shape[0], result, 0)
        for f in ends:
            f()


def local(a_blocks, a_cols, b_blocks, b_rows, c_rows, c_cols):
    smem, vmem = pl.BlockSpec(memory_space=pltpu.SMEM), pl.BlockSpec(memory_space=pltpu.VMEM)
    dma = pltpu.SemaphoreType.DMA
    return pl.pallas_call(
        kernel,
        out_shape=jax.ShapeDtypeStruct((c_rows.shape[0], BS, BS), jnp.float32),
        in_specs=[smem] * 4 + [pl.BlockSpec(memory_space=pl.ANY)] * 2,
        out_specs=vmem,
        scratch_shapes=[
            pltpu.VMEM((64, BS, BS), jnp.float32),
            pltpu.VMEM((32, BS, BS), jnp.float32),
            pltpu.VMEM((65, BS, BS), jnp.bfloat16),
            pltpu.VMEM((65, BS, BS), jnp.bfloat16),
            pltpu.VMEM((8 * BS, 8 * BS), jnp.bfloat16),
            pltpu.VMEM((8 * BS, 8 * BS), jnp.bfloat16),
            pltpu.VMEM((4, 8 * BS, 2 * BS), jnp.bfloat16),
            pltpu.VMEM((32, BS, BS), jnp.float32),
            pltpu.VMEM((64, 1, BS), jnp.int32),
            pltpu.VMEM((16, 1, BS), jnp.int32),
            pltpu.SMEM((64, 1, BS), jnp.int32),
            pltpu.SMEM((16, 1, BS), jnp.int32),
            pltpu.SMEM((8,), jnp.int32),
            pltpu.SMEM((72,), jnp.int32),
            dma((64,)),
            dma((32, CUTS)),
            dma((16,)),
            dma((48,)),
            dma((64,)),
            dma((6 * CUTS,)),
            dma((24 * CUTS,)),
            dma((17,)),
            dma((17,)),
            dma((5,)),
        ],
        compiler_params=pltpu.CompilerParams(collective_id=0, has_side_effects=True, vmem_limit_bytes=62 << 20),
        name="gather_and_multiply",
    )(a_cols, b_rows, c_rows, c_cols, a_blocks, b_blocks)


def solution(mesh):
    in_specs = (
        P(("row", "col"), None, None),
        P(("row", "col")),
        P("row", "col", None, None),
        P("row", "col"),
        P(("row", "col")),
        P(("row", "col")),
    )
    out_specs = P(("row", "col"), None, None)
    return jax.shard_map(local, mesh=mesh, in_specs=in_specs, out_specs=out_specs, check_vma=False)
```

```python
import functools

import jax
import jax.numpy as jnp
from jax import lax
from jax.experimental import pallas as pl
from jax.experimental.pallas import tpu as pltpu
from jax.sharding import PartitionSpec as P

MESH = pl.DeviceIdType.MESH
BS = 128
KSPAN = 32
SLOTS = 8
NZH, NY, NZL, NX = 4, 4, 8, 4
CUTS = 2
ORDER = (
    "a0", "b0", "y", "k1", "a1", "b1", "k2", "a2", "b2", "x0", "k3", "a3",
    "b3", "x1", "k4", "c1", "a4", "b4", "c2", "x2", "s0", "a5", "b5", "c3",
    "x3", "s1", "a6", "c4", "x4", "s2", "p0", "a7", "c5", "x5", "s3", "x6",
    "s4", "c6", "p1", "p3", "x7", "s5", "s6", "s7", "p2", "w",
)


def kernel(
    a_cols,
    b_rows,
    c_rows,
    c_cols,
    a_ref,
    b_ref,
    out_ref,
    abuf,
    bbuf,
    left,
    right,
    akv,
    bkv,
    aks,
    bks,
    first,
    where_is,
    a_recv,
    b_recv,
    az_send,
    ax_send,
    ac_send,
    bz_send,
    by_send,
    k_send,
    k_recv,
    loc,
):
    row, col = lax.axis_index("row"), lax.axis_index("col")
    zh, y = row // NY, row % NY
    zl, x, core = col // (2 * NX), (col // 2) % NX, col % 2

    def at_z(d):
        return (row, ((zl + d) % NZL) * 8 + x * 2 + core)

    def at_x(d):
        return (row, zl * 8 + ((x + d) % NX) * 2 + core)

    def at_core():
        return (row, zl * 8 + x * 2 + 1 - core)

    def at_zh(d):
        return (((zh + d) % NZH) * NY + y, col)

    def at_y(d):
        return (zh * NY + (y + d) % NY, col)

    barrier = pltpu.get_barrier_semaphore()
    partners = [at_z(d) for d in range(1, NZL)] + [at_x(d) for d in range(1, NX)]
    partners += [at_core()] + [at_zh(d) for d in range(1, NZH)] + [at_y(d) for d in range(1, NY)]
    for device in partners:
        pl.semaphore_signal(barrier, inc=1, device_id=device, device_id_type=MESH)
    own = [
        pltpu.make_async_copy(a_ref.at[0], abuf.at[col], loc.at[0]),
        pltpu.make_async_copy(b_ref.at[0, 0], bbuf.at[2 * row], loc.at[1]),
        pltpu.make_async_copy(b_ref.at[1, 0], bbuf.at[2 * row + 1], loc.at[2]),
    ]
    for c in own:
        c.start()
    akv[core * 32 + x * 8 + zl] = jnp.full((1, BS), a_cols[0], jnp.int32)
    lane = lax.broadcasted_iota(jnp.int32, (1, BS), 1)
    bkv[y * 4 + zh] = jnp.where(lane == 0, b_rows[0, 0], b_rows[1, 0])
    left[64] = jnp.zeros((2 * BS, BS), jnp.bfloat16)
    with jax.named_scope("entry"):
        for c in own:
            c.wait()
        pl.semaphore_wait(barrier, len(partners))

    ends = []

    def copy(ref, send, recv, device):
        return pltpu.make_async_remote_copy(
            src_ref=ref, dst_ref=ref, send_sem=send, recv_sem=recv, device_id=device, device_id_type=MESH
        )

    def when(cond, f):
        if cond is None:
            f()
        else:
            pl.when(cond)(f)

    def go(make, cond=None):
        when(cond, lambda: make().start())
        ends.append(lambda: when(cond, lambda: make().wait_send()))

    def landed(ref, sem):
        pltpu.make_async_copy(ref, ref, sem).wait()

    def a_landed(slot):
        landed(abuf.at[slot], a_recv.at[slot])

    def a_z(slot, j, d, cond):
        go(lambda: copy(abuf.at[slot], az_send.at[j], a_recv.at[slot], at_z(d)), cond)

    def a_x(slot, j, cond):
        for n, d in enumerate((1, 3, 2)):
            go(lambda n=n, d=d: copy(abuf.at[slot], ax_send.at[3 * j + n], a_recv.at[slot], at_x(d)), cond)

    def a_core(slot, j, cond):
        go(lambda: copy(abuf.at[slot], ac_send.at[j], a_recv.at[slot], at_core()), cond)

    def line(k, sign):
        z = zl + sign * k
        return jnp.clip(z, 0, NZL - 1), (None if k == 0 else (z >= 0) & (z < NZL))

    def sides(k):
        return (0,) if k == 0 else (-1, 1)

    def number(k, sign):
        return 0 if k == 0 else 2 * k - 1 + (sign > 0)

    def a_line(k):
        for sign in sides(k):
            z, valid = line(k, sign)
            slot = z * 8 + x * 2 + core
            if k > 0:
                when(valid, lambda: a_landed(slot))
            more_right = (zl < NZL - 1) if valid is None else valid & (zl < NZL - 1)
            more_left = (zl > 0) if valid is None else valid & (zl > 0)
            if sign <= 0 and k < NZL - 1:
                a_z(slot, k, 1, more_right)
            if sign >= 0 and k < NZL - 1:
                a_z(slot, 8 + k, -1, more_left)
        for sign in sides(k):
            z, valid = line(k, sign)
            slot = z * 8 + x * 2 + core
            a_x(slot, number(k, sign), valid)
            a_core(slot, number(k, sign), valid)

    def a_from_x(k):
        for sign in sides(k):
            z, valid = line(k, sign)
            for n, d in enumerate((3, 1, 2)):
                slot = z * 8 + ((x + d) % NX) * 2 + core
                when(valid, lambda: a_landed(slot))
                a_core(slot, 16 + 3 * number(k, sign) + n, valid)

    def a_split(k):
        for sign in sides(k):
            z, valid = line(k, sign)

            def whole():
                for n in range(NX):
                    a_landed(z * 8 + n * 2 + 1 - core)

                def one(s, carry):
                    v = abuf[z * 8 + s]
                    hi = v.astype(jnp.bfloat16)
                    left[z * 8 + s, :BS] = hi
                    left[z * 8 + s, BS:] = (v - hi.astype(jnp.float32)).astype(jnp.bfloat16)
                    return carry

                lax.fori_loop(0, SLOTS, one, 0)

            when(valid, whole)

    part = BS // CUTS

    def b_piece(q, i, h):
        return bbuf.at[2 * (((zh + q) % NZH) * NY + y) + i, pl.ds(h * part, part)]

    def b_sem(q, i, h):
        return b_recv.at[2 * (((zh + q) % NZH) * NY + y) + i, h]

    def b_z(q, i, h, d, j):
        return lambda: copy(b_piece(q, i, h), bz_send.at[j], b_sem(q, i, h), at_zh(d))

    state = {"come": 0, "y": 0}

    def b_y(q, i, h):
        for d in (1, 3, 2):
            j = state["y"]
            go(lambda j=j, d=d: copy(b_piece(q, i, h), by_send.at[j], b_sem(q, i, h), at_y(d)))
            state["y"] += 1

    to_right = [(0, i, h) for i in (0, 1) for h in range(CUTS)] + [(-1, 0, h) for h in range(CUTS)]
    to_left = [(0, i, h) for i in (1, 0) for h in range(CUTS)] + [(1, 1, h) for h in range(CUTS)]
    from_left = [(-1, i, h) for i in (0, 1) for h in range(CUTS)] + [(2, 0, h) for h in range(CUTS)]
    from_right = [(1, i, h) for i in (1, 0) for h in range(CUTS)] + [(2, 1, h) for h in range(CUTS)]

    def b_come(count):
        while state["come"] < count:
            for p in (from_left[state["come"]], from_right[state["come"]]):
                landed(b_piece(*p), b_sem(*p))
                b_y(*p)
            state["come"] += 1

    def b_send(k):
        go(b_z(*to_right[k], 1, 2 * k))
        go(b_z(*to_left[k], 3, 2 * k + 1))

    def b_own_y():
        for i in (0, 1):
            for h in range(CUTS):
                b_y(0, i, h)

    sems = {"n": 0}

    def key_go(ref, back, device):
        j = sems["n"]
        sems["n"] += 1
        go(lambda: copy(ref, k_send.at[j], k_recv.at[j], device))
        return lambda: landed(back, k_recv.at[j])

    def keys_1():
        out = []
        for d in range(1, NZL):
            base = core * 32 + x * 8
            out.append(key_go(akv.at[base + zl], akv.at[base + (zl - d) % NZL], at_z(d)))
        for d in range(1, NZH):
            out.append(key_go(bkv.at[y * 4 + zh], bkv.at[y * 4 + (zh - d) % NZH], at_zh(d)))
        return out

    def keys_2():
        out = []
        for d in range(1, NX):
            base = core * 32
            out.append(key_go(akv.at[pl.ds(base + x * 8, 8)], akv.at[pl.ds(base + ((x - d) % NX) * 8, 8)], at_x(d)))
        for d in range(1, NY):
            out.append(key_go(bkv.at[pl.ds(y * 4, 4)], bkv.at[pl.ds(((y - d) % NY) * 4, 4)], at_y(d)))
        return out

    def keys_3():
        return [key_go(akv.at[pl.ds(core * 32, 32)], akv.at[pl.ds((1 - core) * 32, 32)], at_core())]

    def keys_read():
        c0 = pltpu.make_async_copy(akv, aks, loc.at[3])
        c1 = pltpu.make_async_copy(bkv, bks, loc.at[4])
        c0.start()
        c1.start()
        c0.wait()
        c1.wait()

        def one(i, carry):
            keys = [aks[(s % 2) * 32 + (s // 2) * 8 + i, 0, 0] for s in range(SLOTS)]
            past = [lax.rem(k - keys[0] + KSPAN + KSPAN // 2, KSPAN) for k in keys]
            low = functools.reduce(jnp.minimum, past)
            first[i] = lax.rem(keys[0] + low + KSPAN - KSPAN // 2, KSPAN)
            for p in range(SLOTS):
                slot = sum(jnp.where(past[s] - low == p, s, 0) for s in range(SLOTS))
                where_is[i * 9 + p] = i * SLOTS + jnp.minimum(slot, SLOTS - 1)
            where_is[i * 9 + SLOTS] = 64
            return carry

        lax.fori_loop(0, 8, one, 0)

    def column_split(q):
        j = (zh + q) % NZH
        with jax.named_scope(f"column_wait{q}"):
            for d in range(1, NY):
                for i in (0, 1):
                    for h in range(CUTS):
                        slot = 2 * (j * NY + (y + d) % NY) + i
                        landed(bbuf.at[slot, pl.ds(h * part, part)], b_recv.at[slot, h])

        def one(s, carry):
            v = bbuf[j * SLOTS + s]
            hi = v.astype(jnp.bfloat16)
            rows = pl.ds(pl.multiple_of(s * BS, BS), BS)
            right[j, rows, :BS] = hi
            right[j, rows, BS:] = (v - hi.astype(jnp.float32)).astype(jnp.bfloat16)
            return carry

        lax.fori_loop(0, SLOTS, one, 0)

    def pairs():
        def one(t, carry):
            i, j = lax.rem(c_rows[t], 8), lax.rem(c_cols[t], 4)
            at = []
            for s in range(SLOTS):
                key = bks[(s // 2) * 4 + j, 0, s % 2]
                at.append(where_is[i * 9 + jnp.minimum(lax.rem(key - first[i] + KSPAN, KSPAN), SLOTS)])
            total = jnp.zeros((2 * BS, 2 * BS), jnp.float32)
            for s in range(0, SLOTS, 2):
                both = jnp.concatenate([left[at[s]], left[at[s + 1]]], axis=1)
                total += jnp.dot(both, right[j, s * BS : (s + 2) * BS], preferred_element_type=jnp.float32)
            out_ref[t] = total[:BS, :BS] + total[:BS, BS:] + total[BS:, :BS] + total[BS:, BS:]
            return carry

        lax.fori_loop(0, out_ref.shape[0], one, 0)

    steps = {
        "a": a_line,
        "x": a_from_x,
        "s": a_split,
        "b": b_send,
        "c": b_come,
        "y": b_own_y,
        "p": column_split,
        "w": pairs,
    }
    keys = []
    for step in ORDER:
        if step[0] == "k":
            for f in keys:
                f()
            keys = {"1": keys_1, "2": keys_2, "3": keys_3, "4": keys_read}[step[1]]() or []
        else:
            steps[step[0]](*[int(v) for v in step[1:].split(".") if v])

    for f in ends:
        f()


def local(a_blocks, a_cols, b_blocks, b_rows, c_rows, c_cols):
    smem, vmem = pl.BlockSpec(memory_space=pltpu.SMEM), pl.BlockSpec(memory_space=pltpu.VMEM)
    dma = pltpu.SemaphoreType.DMA
    return pl.pallas_call(
        kernel,
        out_shape=jax.ShapeDtypeStruct((c_rows.shape[0], BS, BS), jnp.float32),
        in_specs=[smem] * 4 + [pl.BlockSpec(memory_space=pltpu.HBM)] * 2,
        out_specs=vmem,
        scratch_shapes=[
            pltpu.VMEM((64, BS, BS), jnp.float32),
            pltpu.VMEM((32, BS, BS), jnp.float32),
            pltpu.VMEM((65, 2 * BS, BS), jnp.bfloat16),
            pltpu.VMEM((4, 8 * BS, 2 * BS), jnp.bfloat16),
            pltpu.VMEM((64, 1, BS), jnp.int32),
            pltpu.VMEM((16, 1, BS), jnp.int32),
            pltpu.SMEM((64, 1, BS), jnp.int32),
            pltpu.SMEM((16, 1, BS), jnp.int32),
            pltpu.SMEM((8,), jnp.int32),
            pltpu.SMEM((72,), jnp.int32),
            dma((64,)),
            dma((32, CUTS)),
            dma((16,)),
            dma((48,)),
            dma((64,)),
            dma((6 * CUTS,)),
            dma((24 * CUTS,)),
            dma((17,)),
            dma((17,)),
            dma((5,)),
        ],
        compiler_params=pltpu.CompilerParams(collective_id=0, has_side_effects=True, vmem_limit_bytes=40 << 20),
        name="gather_and_multiply",
    )(a_cols, b_rows, c_rows, c_cols, a_blocks, b_blocks)


def solution(mesh):
    in_specs = (
        P(("row", "col"), None, None),
        P(("row", "col")),
        P("row", "col", None, None),
        P("row", "col"),
        P(("row", "col")),
        P(("row", "col")),
    )
    out_specs = P(("row", "col"), None, None)
    return jax.shard_map(local, mesh=mesh, in_specs=in_specs, out_specs=out_specs, check_vma=False)
```

```python
import functools

import jax
import jax.numpy as jnp
from jax import lax
from jax.experimental import pallas as pl
from jax.experimental.pallas import tpu as pltpu
from jax.sharding import PartitionSpec as P

MESH = pl.DeviceIdType.MESH
BS = 128
KSPAN = 32
SLOTS = 8
NZH, NY, NZL, NX = 4, 4, 8, 4
CUTS = 2
ORDER = (
    "a0", "b0", "k1", "a1", "b1", "k2", "a2", "b2", "x0", "k3", "a3", "y",
    "b3", "x1", "k4", "c1", "a4", "b4", "c2", "x2", "s0", "a5", "b5", "c3",
    "x3", "s1", "a6", "c4", "x4", "s2", "p0", "a7", "c5", "x5", "s3", "x6",
    "s4", "c6", "p1", "p3", "x7", "s5", "s6", "s7", "p2", "w",
)


def kernel(
    a_cols,
    b_rows,
    c_rows,
    c_cols,
    a_ref,
    b_ref,
    out_ref,
    abuf,
    bbuf,
    left,
    right,
    akv,
    bkv,
    aks,
    bks,
    first,
    where_is,
    a_recv,
    b_recv,
    az_send,
    ax_send,
    ac_send,
    bz_send,
    by_send,
    k_send,
    k_recv,
    loc,
):
    row, col = lax.axis_index("row"), lax.axis_index("col")
    zh, y = row // NY, row % NY
    zl, x, core = col // (2 * NX), (col // 2) % NX, col % 2

    def at_z(d):
        return (row, ((zl + d) % NZL) * 8 + x * 2 + core)

    def at_x(d):
        return (row, zl * 8 + ((x + d) % NX) * 2 + core)

    def at_core():
        return (row, zl * 8 + x * 2 + 1 - core)

    def at_zh(d):
        return (((zh + d) % NZH) * NY + y, col)

    def at_y(d):
        return (zh * NY + (y + d) % NY, col)

    barrier = pltpu.get_barrier_semaphore()
    partners = [at_z(d) for d in range(1, NZL)] + [at_x(d) for d in range(1, NX)]
    partners += [at_core()] + [at_zh(d) for d in range(1, NZH)] + [at_y(d) for d in range(1, NY)]
    for device in partners:
        pl.semaphore_signal(barrier, inc=1, device_id=device, device_id_type=MESH)
    own = [
        pltpu.make_async_copy(a_ref.at[0], abuf.at[col], loc.at[0]),
        pltpu.make_async_copy(b_ref.at[0, 0], bbuf.at[2 * row], loc.at[1]),
        pltpu.make_async_copy(b_ref.at[1, 0], bbuf.at[2 * row + 1], loc.at[2]),
    ]
    for c in own:
        c.start()
    akv[core * 32 + x * 8 + zl] = jnp.full((1, BS), a_cols[0], jnp.int32)
    lane = lax.broadcasted_iota(jnp.int32, (1, BS), 1)
    bkv[y * 4 + zh] = jnp.where(lane == 0, b_rows[0, 0], b_rows[1, 0])
    left[64] = jnp.zeros((2 * BS, BS), jnp.bfloat16)
    with jax.named_scope("entry"):
        for c in own:
            c.wait()
        pl.semaphore_wait(barrier, len(partners))

    ends = []

    def copy(ref, send, recv, device):
        return pltpu.make_async_remote_copy(
            src_ref=ref, dst_ref=ref, send_sem=send, recv_sem=recv, device_id=device, device_id_type=MESH
        )

    def when(cond, f):
        if cond is None:
            f()
        else:
            pl.when(cond)(f)

    def go(make, cond=None):
        when(cond, lambda: make().start())
        ends.append(lambda: when(cond, lambda: make().wait_send()))

    def landed(ref, sem):
        pltpu.make_async_copy(ref, ref, sem).wait()

    def a_landed(slot):
        landed(abuf.at[slot], a_recv.at[slot])

    def a_z(slot, j, d, cond):
        go(lambda: copy(abuf.at[slot], az_send.at[j], a_recv.at[slot], at_z(d)), cond)

    def a_x(slot, j, cond):
        for n, d in enumerate((1, 3, 2)):
            go(lambda n=n, d=d: copy(abuf.at[slot], ax_send.at[3 * j + n], a_recv.at[slot], at_x(d)), cond)

    def a_core(slot, j, cond):
        go(lambda: copy(abuf.at[slot], ac_send.at[j], a_recv.at[slot], at_core()), cond)

    def line(k, sign):
        z = zl + sign * k
        return jnp.clip(z, 0, NZL - 1), (None if k == 0 else (z >= 0) & (z < NZL))

    def sides(k):
        return (0,) if k == 0 else (-1, 1)

    def number(k, sign):
        return 0 if k == 0 else 2 * k - 1 + (sign > 0)

    def a_line(k):
        for sign in sides(k):
            z, valid = line(k, sign)
            slot = z * 8 + x * 2 + core
            if k > 0:
                when(valid, lambda: a_landed(slot))
            more_right = (zl < NZL - 1) if valid is None else valid & (zl < NZL - 1)
            more_left = (zl > 0) if valid is None else valid & (zl > 0)
            if sign <= 0 and k < NZL - 1:
                a_z(slot, k, 1, more_right)
            if sign >= 0 and k < NZL - 1:
                a_z(slot, 8 + k, -1, more_left)
        for sign in sides(k):
            z, valid = line(k, sign)
            slot = z * 8 + x * 2 + core
            a_x(slot, number(k, sign), valid)
            a_core(slot, number(k, sign), valid)

    def a_from_x(k):
        for sign in sides(k):
            z, valid = line(k, sign)
            for n, d in enumerate((3, 1, 2)):
                slot = z * 8 + ((x + d) % NX) * 2 + core
                when(valid, lambda: a_landed(slot))
                a_core(slot, 16 + 3 * number(k, sign) + n, valid)

    def a_split(k):
        for sign in sides(k):
            z, valid = line(k, sign)

            def whole():
                for n in range(NX):
                    a_landed(z * 8 + n * 2 + 1 - core)

                def one(s, carry):
                    v = abuf[z * 8 + s]
                    hi = v.astype(jnp.bfloat16)
                    left[z * 8 + s, :BS] = hi
                    left[z * 8 + s, BS:] = (v - hi.astype(jnp.float32)).astype(jnp.bfloat16)
                    return carry

                lax.fori_loop(0, SLOTS, one, 0)

            when(valid, whole)

    part = BS // CUTS

    def b_piece(q, i, h):
        return bbuf.at[2 * (((zh + q) % NZH) * NY + y) + i, pl.ds(h * part, part)]

    def b_sem(q, i, h):
        return b_recv.at[2 * (((zh + q) % NZH) * NY + y) + i, h]

    def b_z(q, i, h, d, j):
        return lambda: copy(b_piece(q, i, h), bz_send.at[j], b_sem(q, i, h), at_zh(d))

    state = {"come": 0, "y": 0}

    def b_y(q, i, h):
        for d in (1, 3, 2):
            j = state["y"]
            go(lambda j=j, d=d: copy(b_piece(q, i, h), by_send.at[j], b_sem(q, i, h), at_y(d)))
            state["y"] += 1

    to_right = [(0, i, h) for i in (0, 1) for h in range(CUTS)] + [(-1, 0, h) for h in range(CUTS)]
    to_left = [(0, i, h) for i in (1, 0) for h in range(CUTS)] + [(1, 1, h) for h in range(CUTS)]
    from_left = [(-1, i, h) for i in (0, 1) for h in range(CUTS)] + [(2, 0, h) for h in range(CUTS)]
    from_right = [(1, i, h) for i in (1, 0) for h in range(CUTS)] + [(2, 1, h) for h in range(CUTS)]

    def b_come(count):
        while state["come"] < count:
            for p in (from_left[state["come"]], from_right[state["come"]]):
                landed(b_piece(*p), b_sem(*p))
                b_y(*p)
            state["come"] += 1

    def b_send(k):
        go(b_z(*to_right[k], 1, 2 * k))
        go(b_z(*to_left[k], 3, 2 * k + 1))

    def b_own_y():
        for i in (0, 1):
            for h in range(CUTS):
                b_y(0, i, h)

    sems = {"n": 0}

    def key_go(ref, back, device):
        j = sems["n"]
        sems["n"] += 1
        go(lambda: copy(ref, k_send.at[j], k_recv.at[j], device))
        return lambda: landed(back, k_recv.at[j])

    def keys_1():
        out = []
        for d in range(1, NZL):
            base = core * 32 + x * 8
            out.append(key_go(akv.at[base + zl], akv.at[base + (zl - d) % NZL], at_z(d)))
        for d in range(1, NZH):
            out.append(key_go(bkv.at[y * 4 + zh], bkv.at[y * 4 + (zh - d) % NZH], at_zh(d)))
        return out

    def keys_2():
        out = []
        for d in range(1, NX):
            base = core * 32
            out.append(key_go(akv.at[pl.ds(base + x * 8, 8)], akv.at[pl.ds(base + ((x - d) % NX) * 8, 8)], at_x(d)))
        for d in range(1, NY):
            out.append(key_go(bkv.at[pl.ds(y * 4, 4)], bkv.at[pl.ds(((y - d) % NY) * 4, 4)], at_y(d)))
        return out

    def keys_3():
        return [key_go(akv.at[pl.ds(core * 32, 32)], akv.at[pl.ds((1 - core) * 32, 32)], at_core())]

    def keys_read():
        c0 = pltpu.make_async_copy(akv, aks, loc.at[3])
        c1 = pltpu.make_async_copy(bkv, bks, loc.at[4])
        c0.start()
        c1.start()
        c0.wait()
        c1.wait()

        def one(i, carry):
            keys = [aks[(s % 2) * 32 + (s // 2) * 8 + i, 0, 0] for s in range(SLOTS)]
            past = [lax.rem(k - keys[0] + KSPAN + KSPAN // 2, KSPAN) for k in keys]
            low = functools.reduce(jnp.minimum, past)
            first[i] = lax.rem(keys[0] + low + KSPAN - KSPAN // 2, KSPAN)
            for p in range(SLOTS):
                slot = sum(jnp.where(past[s] - low == p, s, 0) for s in range(SLOTS))
                where_is[i * 9 + p] = i * SLOTS + jnp.minimum(slot, SLOTS - 1)
            where_is[i * 9 + SLOTS] = 64
            return carry

        lax.fori_loop(0, 8, one, 0)

    def column_split(q):
        j = (zh + q) % NZH
        with jax.named_scope(f"column_wait{q}"):
            for d in range(1, NY):
                for i in (0, 1):
                    for h in range(CUTS):
                        slot = 2 * (j * NY + (y + d) % NY) + i
                        landed(bbuf.at[slot, pl.ds(h * part, part)], b_recv.at[slot, h])

        def one(s, carry):
            v = bbuf[j * SLOTS + s]
            hi = v.astype(jnp.bfloat16)
            rows = pl.ds(pl.multiple_of(s * BS, BS), BS)
            right[j, rows, :BS] = hi
            right[j, rows, BS:] = (v - hi.astype(jnp.float32)).astype(jnp.bfloat16)
            return carry

        lax.fori_loop(0, SLOTS, one, 0)

    def pairs():
        def one(t, carry):
            i, j = lax.rem(c_rows[t], 8), lax.rem(c_cols[t], 4)
            at = []
            for s in range(SLOTS):
                key = bks[(s // 2) * 4 + j, 0, s % 2]
                at.append(where_is[i * 9 + jnp.minimum(lax.rem(key - first[i] + KSPAN, KSPAN), SLOTS)])
            total = jnp.zeros((2 * BS, 2 * BS), jnp.float32)
            for s in range(0, SLOTS, 2):
                both = jnp.concatenate([left[at[s]], left[at[s + 1]]], axis=1)
                total += jnp.dot(both, right[j, s * BS : (s + 2) * BS], preferred_element_type=jnp.float32)
            out_ref[t] = total[:BS, :BS] + total[:BS, BS:] + total[BS:, :BS] + total[BS:, BS:]
            return carry

        lax.fori_loop(0, out_ref.shape[0], one, 0)

    steps = {
        "a": a_line,
        "x": a_from_x,
        "s": a_split,
        "b": b_send,
        "c": b_come,
        "y": b_own_y,
        "p": column_split,
        "w": pairs,
    }
    keys = []
    for step in ORDER:
        if step[0] == "k":
            for f in keys:
                f()
            keys = {"1": keys_1, "2": keys_2, "3": keys_3, "4": keys_read}[step[1]]() or []
        else:
            steps[step[0]](*[int(v) for v in step[1:].split(".") if v])

    for f in ends:
        f()


def local(a_blocks, a_cols, b_blocks, b_rows, c_rows, c_cols):
    smem, vmem = pl.BlockSpec(memory_space=pltpu.SMEM), pl.BlockSpec(memory_space=pltpu.VMEM)
    dma = pltpu.SemaphoreType.DMA
    return pl.pallas_call(
        kernel,
        out_shape=jax.ShapeDtypeStruct((c_rows.shape[0], BS, BS), jnp.float32),
        in_specs=[smem] * 4 + [pl.BlockSpec(memory_space=pltpu.HBM)] * 2,
        out_specs=vmem,
        scratch_shapes=[
            pltpu.VMEM((64, BS, BS), jnp.float32),
            pltpu.VMEM((32, BS, BS), jnp.float32),
            pltpu.VMEM((65, 2 * BS, BS), jnp.bfloat16),
            pltpu.VMEM((4, 8 * BS, 2 * BS), jnp.bfloat16),
            pltpu.VMEM((64, 1, BS), jnp.int32),
            pltpu.VMEM((16, 1, BS), jnp.int32),
            pltpu.SMEM((64, 1, BS), jnp.int32),
            pltpu.SMEM((16, 1, BS), jnp.int32),
            pltpu.SMEM((8,), jnp.int32),
            pltpu.SMEM((72,), jnp.int32),
            dma((64,)),
            dma((32, CUTS)),
            dma((16,)),
            dma((48,)),
            dma((64,)),
            dma((6 * CUTS,)),
            dma((24 * CUTS,)),
            dma((17,)),
            dma((17,)),
            dma((5,)),
        ],
        compiler_params=pltpu.CompilerParams(collective_id=0, has_side_effects=True, vmem_limit_bytes=40 << 20),
        name="gather_and_multiply",
    )(a_cols, b_rows, c_rows, c_cols, a_blocks, b_blocks)


def solution(mesh):
    in_specs = (
        P(("row", "col"), None, None),
        P(("row", "col")),
        P("row", "col", None, None),
        P("row", "col"),
        P(("row", "col")),
        P(("row", "col")),
    )
    out_specs = P(("row", "col"), None, None)
    return jax.shard_map(local, mesh=mesh, in_specs=in_specs, out_specs=out_specs, check_vma=False)
```
